256 devices in a mesh: dom: 32 (over y, x, core), head: 8 (over z).
Axes of the slice: x: 4, y: 4, z: 8, core: 2. Of those that a mesh axis runs over, the one named last changes fastest.
Arguments:
- embeds: bfloat16 [2, 1024, 3584], P(None, 'dom'), may hold values from -6 to 6
- ancestors: int32 [1024], replicated, may hold values from 0 to 1023, as said below
- lengths: int32 [1024], replicated, may hold values from 64 to 256
- kv_cache: bfloat16 [1024, 256, 8, 512], P('dom', None, 'head'), may hold values from -480 to 480, as said below
- attn_gain: float32 [3584], replicated, may hold values from 0.25 to 1.75
- w_query: bfloat16 [3584, 4096], P(None, 'head'), may hold values from -0.09375 to 0.09375
- w_keyval: bfloat16 [3584, 4096], P(None, 'head'), may hold values from -0.09375 to 0.09375
- w_out: bfloat16 [4096, 3584], P('head'), may hold values from -0.09375 to 0.09375
- post_gain: float32 [3584], replicated, may hold values from 0.25 to 1.75
- final_gain: float32 [3584], replicated, may hold values from 0.25 to 1.75
- twist_weight: float32 [3584], replicated, may hold values from -0.09375 to 0.09375
Outputs:
- hidden_out: bfloat16 [2, 1024, 3584], P(None, 'dom')
- twist: float32 [2, 1024], P(None, 'dom')
The draws below stay inside these ranges and needn't reach their ends.
Inputs may be any that keep to these rules, and one draw needn't show every extreme that they name: The particles of one index of dom (an aligned block of 32 particles) have ancestors in exactly 16 distinct aligned blocks, exactly 2 particles in each, and all particles whose ancestors lie in one common aligned block have the same ancestor. `kv_cache`: cached keys and values are finite.
All inputs are finite; a program needn't handle non-finite values.
Results may differ from the reference program's by a relative error of at most 0.012.
The reference program's roundings to bfloat16 on the way (of `normed`, `rotated` and `attended`) count: a program that leaves them out, or rounds other values in their place, can miss the bound.
Values may be sent and summed in bfloat16 or wider, within the bound.
A program may use at most 128 MiB of HBM per device.

```python
import math
import jax
import jax.numpy as jnp
from jax import lax

D = 3584
HD = 256
KVH = 8
QPK = 2
P_DEV = 32
CTX = 256
STEPS = 2
PART = 1024


def draw_ancestors(key, part):
    key = jax.random.fold_in(key, 11)
    keys = jax.random.split(key, 7)
    devices = PART // P_DEV
    picks = devices // 2
    per_source = P_DEV // picks
    order = jax.random.permutation(keys[0], devices)
    boost = jnp.zeros((devices,), jnp.int32).at[order].set(jnp.arange(devices, dtype=jnp.int32) * 4096)
    noise = jax.random.randint(keys[1], (devices, devices), 0, 4096 * devices // 2)
    scores = (noise + boost[None, :]) * devices + jnp.arange(devices, dtype=jnp.int32)[None, :]
    top_scores, picked = lax.top_k(scores, picks)
    shuffle_keys = jax.random.split(keys[2], devices)
    shuffles = jax.vmap(lambda k: jax.random.permutation(k, P_DEV))(shuffle_keys)
    source = jnp.take_along_axis(picked, shuffles // per_source, axis=1)
    heavy = jax.random.randint(keys[4], (devices,), 0, P_DEV)
    others = jax.random.randint(keys[5], (devices, devices), 0, P_DEV)
    coins = jax.random.randint(keys[6], (devices, devices), 0, 2)
    chosen = jnp.where(coins == 1, heavy[None, :], others)
    within = jnp.take_along_axis(chosen, source, axis=1)
    return (source * P_DEV + within).reshape(PART).astype(jnp.int32)


def draw_kv_cache(key, part):
    key = jax.random.fold_in(key, 5)
    base_key = jax.random.fold_in(key, 0)
    values = jnp.clip(jax.random.normal(base_key, (PART, CTX, KVH, 2 * HD), jnp.float32), -6.0, 6.0)
    return values.astype(jnp.bfloat16)


def touch_ends(drawn, own_key, least, largest):
    place = [jax.random.randint(jax.random.fold_in(own_key, axis), (), 0, length) for axis, length in enumerate(drawn.shape)]
    longest = drawn.shape.index(max(drawn.shape))
    next_to = place[:longest] + [(place[longest] + 1) % drawn.shape[longest]] + place[longest + 1:]
    return drawn.at[tuple(place)].set(least).at[tuple(next_to)].set(largest)


def level_of(rng, extent, pieces, least, top_value):
    level = 1.0
    for position, shards_of in pieces:
        heights = jax.random.uniform(jax.random.fold_in(jax.random.fold_in(rng, 6), position), (shards_of,), jnp.float32, least / len(pieces), top_value / len(pieces))
        level = level * jnp.repeat(jnp.exp(heights), extent[position] // shards_of).reshape((-1,) + (1,) * (len(extent) - 1 - position))
    return level


def centred(stream_key, shape, scale, limit, cuts=(), kind=jnp.bfloat16):
    array = jax.random.normal(stream_key, shape, jnp.float32) * scale
    if len(cuts) > 0:
        array = level_of(stream_key, shape, cuts, -0.22, 0.18) * array
    return jnp.clip(array, min=-limit, max=limit).astype(kind)


def setup_inputs(seed: int = 0) -> dict:
    splits = jax.random.split(jax.random.key(seed), 12)
    return {
        "embeds": centred(splits[0], (STEPS, PART, D), 1.0, 6.0, ((1, 32),)),
        "ancestors": draw_ancestors(jax.random.fold_in(splits[11], 71), 0),
        "lengths": touch_ends(jax.random.randint(splits[2], (PART,), CTX // 4, CTX + 1), jax.random.fold_in(splits[2], 1), CTX // 4, CTX).astype(jnp.int32),
        "kv_cache": draw_kv_cache(jax.random.fold_in(splits[11], 71), 0),
        "attn_gain": jnp.clip(1.0 + 0.15 * jax.random.normal(splits[4], (D,), jnp.float32), 0.25, 1.75),
        "w_query": centred(splits[5], (D, KVH * QPK * HD), D ** -0.5, 0.09375, ((1, 8),)),
        "w_keyval": centred(splits[6], (D, KVH * 2 * HD), D ** -0.5, 0.09375, ((1, 8),)),
        "w_out": centred(splits[7], (KVH * QPK * HD, D), (KVH * QPK * HD) ** -0.5, 0.09375, ((0, 8),)),
        "post_gain": jnp.clip(1.0 + 0.15 * jax.random.normal(splits[8], (D,), jnp.float32), 0.25, 1.75),
        "final_gain": jnp.clip(1.0 + 0.15 * jax.random.normal(splits[9], (D,), jnp.float32), 0.25, 1.75),
        "twist_weight": centred(splits[10], (D,), D ** -0.5, 0.09375, (), jnp.float32),
    }


EPSILON = 1e-06
SCORE_SCALE = 0.0625
MASKED_SCORE = -1e+30
LOG_THETA = math.log(10000.0)

def normalize(values, gains):
    mean_square = lax.optimization_barrier(jnp.mean(values * values, axis=-1, keepdims=True))
    return values * lax.rsqrt(mean_square + EPSILON) * gains

def rope_tables(positions, half_dim):
    inverse = jnp.exp(jnp.arange(half_dim, dtype=jnp.float32) * (-LOG_THETA / half_dim))
    angles = positions.astype(jnp.float32)[..., None] * inverse
    return (jnp.cos(angles), jnp.sin(angles))

def rotate(values, cosine, sine):
    half_dim = values.shape[-1] // 2
    first_half = values[..., :half_dim]
    second_half = values[..., half_dim:]
    return jnp.concatenate([first_half * cosine - second_half * sine, second_half * cosine + first_half * sine], axis=-1)

def prefix_partial(queries, kv_block, valid_len):
    head_dim = queries.shape[-1]
    cached_keys = kv_block[..., :head_dim].astype(jnp.float32)
    cached_values = kv_block[..., head_dim:].astype(jnp.float32)
    scores = jnp.einsum('tgrh,cgh->tgrc', queries.astype(jnp.float32), cached_keys) * SCORE_SCALE
    valid = jnp.arange(kv_block.shape[0]) < valid_len
    scores = jnp.where(valid, scores, MASKED_SCORE)
    highest = lax.optimization_barrier(jnp.max(scores, axis=-1))
    expo = jnp.exp(scores - highest[..., None])
    totals = lax.optimization_barrier(jnp.sum(expo, axis=-1))
    rounded = lax.optimization_barrier(expo.astype(jnp.bfloat16)).astype(jnp.float32)
    weighted = jnp.einsum('tgrc,cgh->tgrh', rounded, cached_values)
    return (highest, totals, weighted)

def fresh_partial(queries, new_keys, new_values):
    steps = queries.shape[0]
    scores = jnp.einsum('tpgrh,upgh->tpgru', queries.astype(jnp.float32), new_keys.astype(jnp.float32)) * SCORE_SCALE
    allowed = jnp.arange(steps)[None, :] <= jnp.arange(steps)[:, None]
    scores = jnp.where(allowed[:, None, None, None, :], scores, MASKED_SCORE)
    highest = lax.optimization_barrier(jnp.max(scores, axis=-1))
    expo = jnp.exp(scores - highest[..., None])
    totals = lax.optimization_barrier(jnp.sum(expo, axis=-1))
    rounded = lax.optimization_barrier(expo.astype(jnp.bfloat16)).astype(jnp.float32)
    weighted = jnp.einsum('tpgru,upgh->tpgrh', rounded, new_values.astype(jnp.float32))
    return (highest, totals, weighted)

def merge_partials(cached, fresh):
    high_cached, total_cached, out_cached = cached
    high_fresh, total_fresh, out_fresh = fresh
    highest = jnp.maximum(high_cached, high_fresh)
    cached_factor = jnp.exp(high_cached - highest)
    fresh_factor = jnp.exp(high_fresh - highest)
    denominator = cached_factor * total_cached + fresh_factor * total_fresh
    return (cached_factor[..., None] * out_cached + fresh_factor[..., None] * out_fresh) / denominator[..., None]

def reference(embeds, ancestors, lengths, kv_cache, attn_gain, w_query, w_keyval, w_out, post_gain, final_gain, twist_weight):
    steps, count, width = embeds.shape
    heads = kv_cache.shape[2]
    head_dim = kv_cache.shape[3] // 2
    group = w_query.shape[1] // (heads * head_dim)
    inputs = embeds.astype(jnp.float32)
    normed = normalize(inputs, attn_gain).astype(jnp.bfloat16).reshape(steps * count, width)
    queries = jnp.dot(normed, w_query, preferred_element_type=jnp.float32).reshape(steps, count, heads, group, head_dim)
    keyval = jnp.dot(normed, w_keyval, preferred_element_type=jnp.float32).reshape(steps, count, heads, 2, head_dim)
    parent_len = jnp.take(lengths, ancestors)
    positions = parent_len[None, :] + jnp.arange(steps, dtype=jnp.int32)[:, None]
    cosine, sine = rope_tables(positions, head_dim // 2)
    rotated = rotate(queries, cosine[:, :, None, None, :], sine[:, :, None, None, :]).astype(jnp.bfloat16)
    new_keys = rotate(keyval[:, :, :, 0, :], cosine[:, :, None, :], sine[:, :, None, :]).astype(jnp.bfloat16)
    new_values = keyval[:, :, :, 1, :].astype(jnp.bfloat16)
    rotated, new_keys, new_values = lax.optimization_barrier((rotated, new_keys, new_values))

    def per_particle(item):
        query_rows, parent = item
        kv_block = lax.dynamic_index_in_dim(kv_cache, parent, 0, keepdims=False)
        parent_length = lax.dynamic_index_in_dim(lengths, parent, 0, keepdims=False)
        return prefix_partial(query_rows, kv_block, parent_length)
    highest, totals, weighted = lax.map(per_particle, (jnp.moveaxis(rotated, 1, 0), ancestors))
    cached = (jnp.moveaxis(highest, 0, 1), jnp.moveaxis(totals, 0, 1), jnp.moveaxis(weighted, 0, 1))
    fresh = fresh_partial(rotated, new_keys, new_values)
    attended = merge_partials(cached, fresh).astype(jnp.bfloat16)
    projected = jnp.dot(attended.reshape(steps * count, -1), w_out, preferred_element_type=jnp.float32).reshape(steps, count, width)
    updated = inputs + normalize(projected, post_gain)
    twist = lax.optimization_barrier(jnp.sum(normalize(updated, final_gain) * twist_weight, axis=-1))
    return (updated.astype(jnp.bfloat16), twist)
```

```python
import functools
import math

import jax
import jax.numpy as jnp
from jax import lax
from jax.experimental import pallas as pl
from jax.experimental.pallas import tpu as pltpu
from jax.sharding import PartitionSpec as P

EPSILON = 1e-06
SCORE_SCALE = 0.0625
MASKED_SCORE = -1e30
LOG_THETA = math.log(10000.0)
MESH = pl.DeviceIdType.MESH
F32 = jnp.float32
BF16 = jnp.bfloat16
CHUNKS = 7
WINDOW = 5


def iota(shape, dim):
    return lax.broadcasted_iota(jnp.int32, shape, dim)


def dot(a, b):
    return jnp.dot(a, b, preferred_element_type=F32)


def dot_t(a, b):
    return lax.dot_general(a, b, (((1,), (1,)), ((), ())), preferred_element_type=F32)


def split3(x):
    high = x.astype(BF16).astype(F32)
    rest = x - high
    mid = rest.astype(BF16).astype(F32)
    return (high, mid, rest - mid)


def kernel(
    grid3, anc_h, len_h, table_h, emb_h, gain_h, post_h, final_h, twist_h,
    wq_h, wkv_h, wo_h, kv_h, g_recv,
    anc_s, len_s, anc_v, gains, emb_b, x32, nrm, wq, wkv, wo, kv, a_v, a_s, q_send, q_recv, r_send, r_recv,
    rs_send, rs_mid, rs_half, rs_sum, rs_recv, g_send, g_mid,
    index_sem, gain_sem, emb_sem, w_sem, wo_sem, kv_sem, a_sem, q_ssem, q_rsem, r_ssem, r_rsem,
    rs_ssem, rs_rsem, g_ssem, g_rsem, own_sem,
):
    ny, nx, nc = grid3
    peers = ny * nx * nc
    local = peers
    heads = rs_send.shape[0]
    rows, width = emb_b.shape
    half = width // 2
    hd = kv.shape[2] // 2
    ctx = kv.shape[1]
    me = lax.axis_index("dom")
    head = lax.axis_index("head")
    my_y, my_x, my_c = me // (nx * nc), (me // nc) % nx, me % nc

    def ahead(i):
        y = (my_y + i // (nx * nc)) % ny
        x = (my_x + (i // nc) % nx) % nx
        return (y * nx + x) * nc + (my_c + i % nc) % nc

    def behind(i):
        y = (my_y + ny - i // (nx * nc)) % ny
        x = (my_x + nx - (i // nc) % nx) % nx
        return (y * nx + x) * nc + (my_c + nc - i % nc) % nc

    index_copies = [
        pltpu.make_async_copy(src, dst, index_sem.at[k])
        for k, (src, dst) in enumerate(((anc_h, anc_s), (len_h, len_s), (table_h, anc_v)))
    ]
    for copy in index_copies:
        copy.start()
    emb_copy = pltpu.make_async_copy(emb_h, emb_b, emb_sem)
    emb_copy.start()
    gain_copies = [
        pltpu.make_async_copy(src, gains.at[k, 0], gain_sem.at[k])
        for k, src in enumerate((gain_h, post_h, final_h, twist_h))
    ]
    for copy in gain_copies:
        copy.start()
    depth = width // CHUNKS
    w_copies = []
    for c in range(CHUNKS):
        part = pl.ds(c * depth, depth)
        pair = (
            pltpu.make_async_copy(wq_h.at[part], wq.at[part], w_sem.at[0, c]),
            pltpu.make_async_copy(wkv_h.at[part], wkv.at[part], w_sem.at[1, c]),
        )
        w_copies.append(pair)
    for pair in w_copies[:WINDOW]:
        for copy in pair:
            copy.start()
    kv_copy = pltpu.make_async_copy(kv_h, kv, kv_sem)
    wo_copy = pltpu.make_async_copy(wo_h, wo, wo_sem)

    barrier = pltpu.get_barrier_semaphore()

    def greet_dom(i, carry):
        pl.semaphore_signal(barrier, inc=1, device_id={"dom": ahead(i)}, device_id_type=MESH)
        return carry

    def greet_head(i, carry):
        pl.semaphore_signal(
            barrier, inc=1, device_id={"head": (head + i) % heads}, device_id_type=MESH
        )
        return carry

    lax.fori_loop(1, peers, greet_dom, 0)
    lax.fori_loop(1, heads, greet_head, 0)

    for copy in index_copies:
        copy.wait()
    table = anc_v[...]
    lines, lanes = table.shape
    lane = iota((lines, lanes), 1)
    hit = jnp.where(table // local == me, table % local, 0)
    picked = jnp.zeros((lines, lanes), jnp.int32)
    for q in range(lanes // local):
        best = jnp.max(jnp.where(lane // local == q, hit, 0), axis=1, keepdims=True)
        picked = jnp.where(lane == q, best, picked)
    a_v[...] = picked
    a_copy = pltpu.make_async_copy(a_v, a_s, a_sem)
    a_copy.start()

    sub = iota((local, 128), 0)
    lane = iota((local, 128), 1)
    source_col = jnp.zeros((local, 128), jnp.int32)
    source_row = jnp.zeros((local, 128), jnp.int32)
    length = jnp.zeros((local, 128), jnp.int32)
    for p in range(local):
        parent = anc_s[me * local + p]
        block = parent // local
        source_col = jnp.where(sub == p, block, source_col)
        source_row = jnp.where(lane % local == p, block, source_row)
        length = jnp.where(sub == p, len_s[parent], length)
    same = source_col == source_row
    rank_row = jnp.sum(jnp.where(same & (sub < lane % local), 1, 0), axis=0, keepdims=True)
    rank_col = jnp.sum(
        jnp.where(same & (lane < sub) & (lane < local), 1, 0), axis=1, keepdims=True
    )
    count = 4 * local
    turn = iota((1, count), 1) // local
    base_row = (source_row[0:1] * 8 + rank_row * 4)[:, :count]
    target_q = base_row + 2 * (turn % 2) + turn // 2
    target_n = source_row[0:1, :count] * 8 + 2 * rank_row[:, :count] + turn % 2 + 4 * (turn // 2)
    slot_row = iota((8 * peers, count), 0)
    gather_q = jnp.where(slot_row == target_q, 1.0, 0.0).astype(BF16)
    gather_n = jnp.where(slot_row == target_n, 1.0, 0.0).astype(BF16)
    base_col = source_col[:, 0:1] * 8 + rank_col * 4
    target_col = jnp.concatenate([base_col + (2 * t + r) for r in range(2) for t in range(2)], 0)
    scatter = jnp.where(iota((count, 8 * peers), 1) == target_col, 1.0, 0.0).astype(BF16)

    position = jnp.concatenate([length, length + 1], axis=0)[:, : hd // 2].astype(F32)
    inverse = jnp.exp(iota((1, hd // 2), 1).astype(F32) * (-LOG_THETA / (hd // 2)))
    angles = position * inverse
    cosine, sine = jnp.cos(angles), jnp.sin(angles)

    def rope(v):
        a, b = v[:, : hd // 2], v[:, hd // 2 :]
        return jnp.concatenate([a * cosine - b * sine, b * cosine + a * sine], axis=1)

    emb_copy.wait()
    for copy in gain_copies:
        copy.wait()
    attn_gain, post_gain, final_gain, twist_weight = (gains.at[k] for k in range(4))

    def norm_rows(i, carry):
        at = pl.ds(pl.multiple_of(i * 16, 16), 16)
        x = emb_b[at, :].astype(F32)
        x32[at, :] = x
        scale = lax.rsqrt(jnp.mean(x * x, axis=1, keepdims=True) + EPSILON)
        nrm[at, :] = (x * scale * attn_gain[...]).astype(BF16)
        return carry

    lax.fori_loop(0, rows // 16, norm_rows, 0)

    queries = jnp.zeros((rows, 2 * hd), F32)
    keyval = jnp.zeros((rows, 2 * hd), F32)
    for c in range(CHUNKS):
        part = slice(c * depth, (c + 1) * depth)
        for copy in w_copies[c]:
            copy.wait()
        if c + WINDOW < CHUNKS:
            for copy in w_copies[c + WINDOW]:
                copy.start()
        queries += dot(nrm[:, part], wq[part, :])
        keyval += dot(nrm[:, part], wkv[part, :])

    kv_copy.start()
    wo_copy.start()

    rotated = jnp.concatenate([rope(queries[:, :hd]), rope(queries[:, hd:])], axis=0)
    fresh = jnp.concatenate([rope(keyval[:, :hd]), keyval[:, hd:]], axis=0)
    q_send[:, :8] = dot(gather_q, rotated.astype(BF16)).reshape(peers, 8, hd).astype(BF16)
    q_send[:, 8:] = dot(gather_n, fresh.astype(BF16)).reshape(peers, 8, hd).astype(BF16)

    def q_copy(i, src, dst, dev):
        return pltpu.make_async_remote_copy(
            src_ref=q_send.at[src], dst_ref=q_recv.at[dst], send_sem=q_ssem.at[i],
            recv_sem=q_rsem.at[dst], device_id={"dom": dev}, device_id_type=MESH,
        )

    pl.semaphore_wait(barrier, peers + heads - 2)

    def q_start(i, carry):
        to = ahead(i)
        q_copy(to, to, me, to).start()
        return carry

    lax.fori_loop(1, peers, q_start, 0)
    q_recv[me] = q_send[me]

    a_copy.wait()
    kv_copy.wait()

    def r_copy(i, src, dst, dev):
        return pltpu.make_async_remote_copy(
            src_ref=r_send.at[src], dst_ref=r_recv.at[dst], send_sem=r_ssem.at[i],
            recv_sem=r_rsem.at[dst], device_id={"dom": dev}, device_id_type=MESH,
        )

    per_line = lanes // local
    lane8 = iota((8, ctx), 1)
    row, col = iota((128, 128), 0), iota((128, 128), 1)
    new = col % 16 - 8
    allowed = (row // 16 == col // 16) & (new >= 0) & (new < 4)
    allowed &= ((row % 8) // 4 == new // 2) & (new % 2 <= (row % 4) // 2)

    def attend(group, carry):
        def q_wait(slot, c):
            @pl.when(slot != me)
            def _():
                q_copy(slot, me, slot, slot).wait_recv()

            return c

        lax.fori_loop(group * 8, group * 8 + 8, q_wait, 0)
        slots, parents, scores, messages = [], [], [], []
        for j in range(8):
            slot = group * 8 + j
            parent = a_s[slot // per_line, slot % per_line]
            message = q_recv[slot]
            score = dot_t(message, kv[parent, :, :hd])[:8] * SCORE_SCALE
            scores.append(jnp.where(lane8 < len_s[me * local + parent], score, MASKED_SCORE))
            slots.append(slot)
            parents.append(parent)
            messages.append(message)
        score = jnp.concatenate(scores, axis=0)
        high_c = jnp.max(score, axis=1, keepdims=True)
        expo = jnp.exp(score - high_c)
        total_c = jnp.sum(expo, axis=1, keepdims=True)
        message = jnp.concatenate(messages, axis=0)
        fresh = jnp.where(allowed, dot_t(message, message) * SCORE_SCALE, MASKED_SCORE)
        high_n = jnp.max(fresh, axis=1, keepdims=True)
        expo_n = jnp.exp(fresh - high_n)
        total_n = jnp.sum(expo_n, axis=1, keepdims=True)
        out_n = dot(pltpu.roll(expo_n, 4, 1).astype(BF16), message)

        def queries_of(v):
            return v.reshape(8, 16, v.shape[1])[:, :8].reshape(64, v.shape[1])

        high_n, total_n, out_n = queries_of(high_n), queries_of(total_n), queries_of(out_n)
        highest = jnp.maximum(high_c, high_n)
        factor_c = jnp.exp(high_c - highest)
        factor_n = jnp.exp(high_n - highest)
        total = factor_c * total_c + factor_n * total_n
        for j in range(8):
            at = slice(8 * j, 8 * j + 8)
            out = dot(expo[at].astype(BF16), kv[parents[j], :, hd:])
            out = (factor_c[at] * out + factor_n[at] * out_n[at]) / total[at]
            r_send[slots[j]] = jnp.concatenate(
                [out[:, : hd // 2], out[:, hd // 2 :]], axis=0
            ).astype(BF16)

        def r_start(slot, c):
            @pl.when(slot != me)
            def _():
                r_copy(slot, slot, me, slot).start()

            return c

        lax.fori_loop(group * 8, group * 8 + 8, r_start, 0)
        return carry

    lax.fori_loop(0, peers // 8, attend, 0)
    r_recv[me] = r_send[me]

    def r_wait(i, carry):
        r_copy(i, me, ahead(i), ahead(i)).wait_recv()
        return carry

    lax.fori_loop(1, peers, r_wait, 0)

    back = r_recv[...].astype(F32)
    back = jnp.concatenate(
        [back[:, :8].reshape(8 * peers, hd // 2), back[:, 8:].reshape(8 * peers, hd // 2)], axis=1
    ).astype(BF16)
    attended = dot(scatter, back)
    attended = jnp.concatenate([attended[:rows], attended[rows:]], axis=1).astype(BF16)

    wo_copy.wait()
    step = 256
    for c in range(0, half, step):
        low = dot(attended, wo[:, c : c + step]).reshape(heads, 8, step)
        upper = dot(attended, wo[:, half + c : half + c + step]).reshape(heads, 8, step)
        rs_send[:, :, c : c + step] = jnp.concatenate([low, upper], axis=1).astype(BF16)

    quarter = half // 2
    part = (pl.ds(0, quarter), pl.ds(quarter, half - quarter))

    def around(d):
        return (head + heads + d) % heads

    def to_head(k, src, dst, send_sem, recv_sem, d):
        return pltpu.make_async_remote_copy(
            src_ref=src, dst_ref=dst, send_sem=send_sem.at[k], recv_sem=recv_sem.at[k],
            device_id={"head": around(d)}, device_id_type=MESH,
        )

    def rs_copy(k, src, dst, d):
        return to_head(k, src, dst, rs_ssem, rs_rsem, d)

    ways = ((0, 1), (1, -1))
    plain = [
        rs_copy(k, rs_send.at[around(3 * d), :, part[1 - k]], rs_mid.at[k, :, part[1 - k]], d)
        for k, d in ways
    ]
    fourth = [rs_copy(2 + k, rs_send.at[around(4), :, part[k]], rs_half.at[k], 2 * d) for k, d in ways]
    third = [
        rs_copy(4 + k, rs_send.at[around(3 * d), :, part[k]], rs_mid.at[k, :, part[k]], d)
        for k, d in ways
    ]
    direct = [rs_copy(6 + k, rs_send.at[around(d)], rs_recv.at[k], d) for k, d in ways]
    for copy in plain + fourth + third + direct:
        copy.start()
    late = []

    def hand_on(n, k, d, at, more):
        block = rs_send[around(2 * d), :, at].astype(F32) + rs_mid[k, :, at].astype(F32)
        if more:
            block += rs_half[k].astype(F32)
        rs_sum[k, :, at] = block.astype(BF16)
        copy = rs_copy(n, rs_sum.at[k, :, at], rs_recv.at[2 + k, :, at], 2 * d)
        copy.start()
        late.append(copy)

    for k, d in ways:
        plain[k].wait_recv()
        hand_on(8 + k, k, d, part[1 - k], False)
    for k, d in ways:
        fourth[k].wait_recv()
        third[k].wait_recv()
        hand_on(10 + k, k, d, part[k], True)
    for copy in direct:
        copy.wait_recv()
    projected = rs_send[head].astype(F32) + rs_recv[0].astype(F32) + rs_recv[1].astype(F32)
    for copy in late:
        copy.wait_recv()
    projected += rs_recv[2].astype(F32) + rs_recv[3].astype(F32)

    low, upper = projected[:8], projected[8:]

    def row_scale(a, b):
        square = jnp.sum(a * a, axis=1, keepdims=True) + jnp.sum(b * b, axis=1, keepdims=True)
        return lax.rsqrt(square * (1.0 / width) + EPSILON)

    mine = pl.ds(pl.multiple_of(head * 8, 8), 8)
    scale = row_scale(low, upper)
    low = x32[mine, :half] + low * scale * post_gain[:, :half]
    upper = x32[mine, half:] + upper * scale * post_gain[:, half:]
    scale = row_scale(low, upper)
    twist = jnp.sum(
        low * scale * final_gain[:, :half] * twist_weight[:, :half], axis=1, keepdims=True
    ) + jnp.sum(
        upper * scale * final_gain[:, half:] * twist_weight[:, half:], axis=1, keepdims=True
    )
    lane = iota((8, 128), 1)
    coded = jnp.zeros((8, 128), F32)
    for k, value in enumerate(split3(twist)):
        coded = jnp.where(lane == k, value, coded)
    g_send[:, :half] = jnp.concatenate([low, upper], axis=0).astype(BF16)
    g_send[:, half:] = jnp.concatenate([coded, jnp.zeros((8, 128), F32)], axis=0).astype(BF16)

    def g_copy(k, src, dst, d):
        return to_head(k, src, dst, g_ssem, g_rsem, d)

    part = (pl.ds(0, quarter), pl.ds(quarter, half + 128 - quarter))
    first = [g_copy(k, g_send.at[:, part[k]], g_mid.at[k, :, part[k]], 2 * d) for k, d in ways]
    first += [
        g_copy(2 + k, g_send.at[:, part[1 - k]], g_mid.at[k, :, part[1 - k]], 2 * d)
        for k, d in ways
    ]
    first += [g_copy(4 + k, g_send, g_recv.at[head], d) for k, d in ways]
    for copy in first:
        copy.start()
    own = [pltpu.make_async_copy(g_send, g_recv.at[head], own_sem.at[4])]
    own[0].start()
    second = []
    for n in range(4):
        k, d = ways[n % 2]
        at = part[k] if n < 2 else part[1 - k]
        first[n].wait_recv()
        here, there = g_mid.at[k, :, at], g_recv.at[around(-2 * d), :, at]
        new = [g_copy(6 + k, here, there, 2 * d)] if n < 2 else []
        new.append(g_copy(8 + n, here, there, d))
        for copy in new:
            copy.start()
        second += new
        own.append(pltpu.make_async_copy(here, there, own_sem.at[n]))
        own[-1].start()
    for copy in first[4:] + second:
        copy.wait_recv()
    for copy in own:
        copy.wait()

    def finish_dom(i, carry):
        to = ahead(i)
        q_copy(to, me, me, to).wait_send()
        r_copy(to, me, me, to).wait_send()
        return carry

    lax.fori_loop(1, peers, finish_dom, 0)
    for copy in plain + fourth + third + direct + late + first + second:
        copy.wait_send()


def order_rows(g_ref, out_v, twist_v):
    heads, half = g_ref.shape[0], g_ref.shape[2] - 128
    steps, local = twist_v.shape
    rows = steps * local
    for j in range(0, heads, 2):
        pair = [g_ref[k, :, :half].astype(F32) for k in (j, j + 1)]
        at = slice(8 * j, 8 * j + 16)
        out_v[at, :half] = jnp.concatenate([v[:8] for v in pair], axis=0).astype(BF16)
        out_v[at, half:] = jnp.concatenate([v[8:] for v in pair], axis=0).astype(BF16)
    coded = jnp.concatenate([g_ref[k, :, half:].astype(F32)[:8] for k in range(heads)], axis=0)
    twist = coded[:, 0:1] + coded[:, 1:2] + coded[:, 2:3]
    spread = jnp.where(iota((rows, 128), 0) % local == iota((rows, 128), 1), twist, 0.0)
    twist_v[...] = jnp.sum(spread.reshape(steps, local, 128), axis=1)[:, :local]


def per_device(
    grid3, embeds, ancestors, lengths, kv_cache, attn_gain, w_query, w_keyval, w_out,
    post_gain, final_gain, twist_weight,
):
    steps, local, width = embeds.shape
    ctx, hd2 = kv_cache.shape[1], kv_cache.shape[3]
    peers = lax.axis_size("dom")
    heads = lax.axis_size("head")
    rows = steps * local
    half = width // 2
    lanes = min(128, ancestors.shape[0])
    lines = ancestors.shape[0] // lanes
    vmem = pl.BlockSpec(memory_space=pltpu.VMEM)
    hbm = pl.BlockSpec(memory_space=pltpu.HBM)
    dma = pltpu.SemaphoreType.DMA
    gathered = pl.pallas_call(
        functools.partial(kernel, grid3),
        out_shape=jax.ShapeDtypeStruct((heads, 16, half + 128), BF16),
        in_specs=[hbm, hbm, hbm, hbm, hbm, hbm, hbm, hbm, hbm, hbm, hbm, hbm],
        out_specs=hbm,
        scratch_shapes=[
            pltpu.SMEM(ancestors.shape, jnp.int32),
            pltpu.SMEM(lengths.shape, jnp.int32),
            pltpu.VMEM((lines, lanes), jnp.int32),
            pltpu.VMEM((4, 1, width), F32),
            pltpu.VMEM((rows, width), BF16),
            pltpu.VMEM((rows, width), F32),
            pltpu.VMEM((rows, width), BF16),
            pltpu.VMEM(w_query.shape, BF16),
            pltpu.VMEM(w_keyval.shape, BF16),
            pltpu.VMEM(w_out.shape, BF16),
            pltpu.VMEM((local, ctx, hd2), BF16),
            pltpu.VMEM((lines, lanes), jnp.int32),
            pltpu.SMEM((lines, lanes), jnp.int32),
            pltpu.VMEM((peers, 16, hd2 // 2), BF16),
            pltpu.VMEM((peers, 16, hd2 // 2), BF16),
            pltpu.VMEM((peers, 16, hd2 // 4), BF16),
            pltpu.VMEM((peers, 16, hd2 // 4), BF16),
            pltpu.VMEM((heads, 16, half), BF16),
            pltpu.VMEM((2, 16, half), BF16),
            pltpu.VMEM((2, 16, half // 2), BF16),
            pltpu.VMEM((2, 16, half), BF16),
            pltpu.VMEM((4, 16, half), BF16),
            pltpu.VMEM((16, half + 128), BF16),
            pltpu.VMEM((2, 16, half + 128), BF16),
            dma((3,)), dma((4,)), dma, dma((2, CHUNKS)), dma, dma, dma,
            dma((peers,)), dma((peers,)), dma((peers,)), dma((peers,)),
            dma((12,)), dma((12,)), dma((12,)), dma((12,)), dma((5,)),
        ],
        compiler_params=pltpu.CompilerParams(
            collective_id=0, has_side_effects=True, vmem_limit_bytes=56 * 1024 * 1024
        ),
    )(
        ancestors, lengths, ancestors.reshape(lines, lanes), embeds.reshape(rows, width),
        attn_gain, post_gain,
        final_gain, twist_weight,
        w_query, w_keyval, w_out, kv_cache.reshape(local, ctx, hd2),
    )
    hidden, twist = pl.pallas_call(
        order_rows,
        out_shape=(
            jax.ShapeDtypeStruct((rows, width), BF16),
            jax.ShapeDtypeStruct((steps, local), F32),
        ),
        in_specs=[vmem],
        out_specs=(vmem, vmem),
        compiler_params=pltpu.CompilerParams(vmem_limit_bytes=56 * 1024 * 1024),
    )(gathered)
    return (hidden.reshape(steps, local, width), twist)


def solution(mesh):
    side = math.isqrt(mesh.shape["dom"] // 2)
    grid3 = (mesh.shape["dom"] // (2 * side), side, 2)
    in_specs = (
        P(None, "dom", None), P(), P(), P("dom", None, "head", None), P(), P(None, "head"),
        P(None, "head"), P("head", None), P(), P(), P(),
    )
    out_specs = (P(None, "dom", None), P(None, "dom"))
    return jax.shard_map(
        functools.partial(per_device, grid3), mesh=mesh, in_specs=in_specs, out_specs=out_specs,
        check_vma=False,
    )
```

```python
import functools
import math

import jax
import jax.numpy as jnp
from jax import lax
from jax.experimental import pallas as pl
from jax.experimental.pallas import tpu as pltpu
from jax.sharding import PartitionSpec as P

EPSILON = 1e-06
SCORE_SCALE = 0.0625
MASKED_SCORE = -1e30
LOG_THETA = math.log(10000.0)
MESH = pl.DeviceIdType.MESH
F32 = jnp.float32
BF16 = jnp.bfloat16
CHUNKS = 2


def iota(shape, dim):
    return lax.broadcasted_iota(jnp.int32, shape, dim)


def dot(a, b):
    return jnp.dot(a, b, preferred_element_type=F32)


def dot_t(a, b):
    return lax.dot_general(a, b, (((1,), (1,)), ((), ())), preferred_element_type=F32)


def split3(x):
    high = x.astype(BF16).astype(F32)
    rest = x - high
    mid = rest.astype(BF16).astype(F32)
    return (high, mid, rest - mid)


def kernel(
    grid3, anc_h, len_h, table_h, emb_h, gain_h, post_h, final_h, twist_h,
    wq_h, wkv_h, wo_h, kv_h, g_recv,
    anc_s, len_s, anc_v, gains, emb_b, x32, nrm, wq, wkv, wo, kv, a_v, a_s, q_send, q_recv, r_send, r_recv,
    rs_send, rs_mid, rs_half, rs_sum, rs_recv, g_send, g_mid,
    index_sem, gain_sem, emb_sem, w_sem, wo_sem, kv_sem, a_sem, q_ssem, q_rsem, r_ssem, r_rsem,
    rs_ssem, rs_rsem, g_ssem, g_rsem, own_sem,
):
    ny, nx, nc = grid3
    peers = ny * nx * nc
    local = peers
    heads = rs_send.shape[0]
    rows, width = emb_b.shape
    half = width // 2
    hd = kv.shape[2] // 2
    ctx = kv.shape[1]
    me = lax.axis_index("dom")
    head = lax.axis_index("head")
    my_y, my_x, my_c = me // (nx * nc), (me // nc) % nx, me % nc

    def ahead(i):
        y = (my_y + i // (nx * nc)) % ny
        x = (my_x + (i // nc) % nx) % nx
        return (y * nx + x) * nc + (my_c + i % nc) % nc

    def behind(i):
        y = (my_y + ny - i // (nx * nc)) % ny
        x = (my_x + nx - (i // nc) % nx) % nx
        return (y * nx + x) * nc + (my_c + nc - i % nc) % nc

    index_copies = [
        pltpu.make_async_copy(src, dst, index_sem.at[k])
        for k, (src, dst) in enumerate(((anc_h, anc_s), (len_h, len_s), (table_h, anc_v)))
    ]
    for copy in index_copies:
        copy.start()
    emb_copy = pltpu.make_async_copy(emb_h, emb_b, emb_sem)
    emb_copy.start()
    gain_copies = [
        pltpu.make_async_copy(src, gains.at[k, 0], gain_sem.at[k])
        for k, src in enumerate((gain_h, post_h, final_h, twist_h))
    ]
    for copy in gain_copies:
        copy.start()
    depth = width // CHUNKS
    w_copies = []
    for k, (src, dst) in enumerate(((wq_h, wq), (wkv_h, wkv))):
        part = [pl.ds(c * depth, depth) for c in range(CHUNKS)]
        w_copies.append(
            [pltpu.make_async_copy(src.at[p], dst.at[p], w_sem.at[k, c]) for c, p in enumerate(part)]
        )
    for copy in w_copies[0]:
        copy.start()
    kv_copy = pltpu.make_async_copy(kv_h, kv, kv_sem)
    wo_copy = pltpu.make_async_copy(wo_h, wo, wo_sem)

    barrier = pltpu.get_barrier_semaphore()

    def greet_dom(i, carry):
        pl.semaphore_signal(barrier, inc=1, device_id={"dom": ahead(i)}, device_id_type=MESH)
        return carry

    def greet_head(i, carry):
        pl.semaphore_signal(
            barrier, inc=1, device_id={"head": (head + i) % heads}, device_id_type=MESH
        )
        return carry

    lax.fori_loop(1, peers, greet_dom, 0)
    lax.fori_loop(1, heads, greet_head, 0)

    for copy in index_copies:
        copy.wait()
    table = anc_v[...]
    lines, lanes = table.shape
    lane = iota((lines, lanes), 1)
    hit = jnp.where(table // local == me, table % local, 0)
    picked = jnp.zeros((lines, lanes), jnp.int32)
    for q in range(lanes // local):
        best = jnp.max(jnp.where(lane // local == q, hit, 0), axis=1, keepdims=True)
        picked = jnp.where(lane == q, best, picked)
    a_v[...] = picked
    a_copy = pltpu.make_async_copy(a_v, a_s, a_sem)
    a_copy.start()

    sub = iota((local, 128), 0)
    lane = iota((local, 128), 1)
    source_col = jnp.zeros((local, 128), jnp.int32)
    source_row = jnp.zeros((local, 128), jnp.int32)
    length = jnp.zeros((local, 128), jnp.int32)
    for p in range(local):
        parent = anc_s[me * local + p]
        block = parent // local
        source_col = jnp.where(sub == p, block, source_col)
        source_row = jnp.where(lane % local == p, block, source_row)
        length = jnp.where(sub == p, len_s[parent], length)
    same = source_col == source_row
    rank_row = jnp.sum(jnp.where(same & (sub < lane % local), 1, 0), axis=0, keepdims=True)
    rank_col = jnp.sum(
        jnp.where(same & (lane < sub) & (lane < local), 1, 0), axis=1, keepdims=True
    )
    count = 4 * local
    turn = iota((1, count), 1) // local
    base_row = (source_row[0:1] * 8 + rank_row * 4)[:, :count]
    target_q = base_row + 2 * (turn % 2) + turn // 2
    target_n = source_row[0:1, :count] * 8 + 2 * rank_row[:, :count] + turn % 2 + 4 * (turn // 2)
    slot_row = iota((8 * peers, count), 0)
    gather_q = jnp.where(slot_row == target_q, 1.0, 0.0).astype(BF16)
    gather_n = jnp.where(slot_row == target_n, 1.0, 0.0).astype(BF16)
    base_col = source_col[:, 0:1] * 8 + rank_col * 4
    target_col = jnp.concatenate([base_col + (2 * t + r) for r in range(2) for t in range(2)], 0)
    scatter = jnp.where(iota((count, 8 * peers), 1) == target_col, 1.0, 0.0).astype(BF16)

    position = jnp.concatenate([length, length + 1], axis=0)[:, : hd // 2].astype(F32)
    inverse = jnp.exp(iota((1, hd // 2), 1).astype(F32) * (-LOG_THETA / (hd // 2)))
    angles = position * inverse
    cosine, sine = jnp.cos(angles), jnp.sin(angles)

    def rope(v):
        a, b = v[:, : hd // 2], v[:, hd // 2 :]
        return jnp.concatenate([a * cosine - b * sine, b * cosine + a * sine], axis=1)

    for copy in w_copies[1]:
        copy.start()
    emb_copy.wait()
    for copy in gain_copies:
        copy.wait()
    attn_gain, post_gain, final_gain, twist_weight = (gains.at[k] for k in range(4))

    def norm_rows(i, carry):
        at = pl.ds(pl.multiple_of(i * 16, 16), 16)
        x = emb_b[at, :].astype(F32)
        x32[at, :] = x
        scale = lax.rsqrt(jnp.mean(x * x, axis=1, keepdims=True) + EPSILON)
        nrm[at, :] = (x * scale * attn_gain[...]).astype(BF16)
        return carry

    lax.fori_loop(0, rows // 16, norm_rows, 0)

    @pl.when(head < heads)
    def _():
        for copy in w_copies[0]:
            copy.wait()
        queries = dot(nrm[...], wq[...])
        rotated = jnp.concatenate([rope(queries[:, :hd]), rope(queries[:, hd:])], axis=0)
        q_send[:, :8] = dot(gather_q, rotated.astype(BF16)).reshape(peers, 8, hd).astype(BF16)

    for copy in w_copies[1]:
        copy.wait()
    kv_copy.start()
    wo_copy.start()
    keyval = dot(nrm[...], wkv[...])
    fresh = jnp.concatenate([rope(keyval[:, :hd]), keyval[:, hd:]], axis=0)
    q_send[:, 8:] = dot(gather_n, fresh.astype(BF16)).reshape(peers, 8, hd).astype(BF16)

    def q_copy(i, src, dst, dev):
        return pltpu.make_async_remote_copy(
            src_ref=q_send.at[src], dst_ref=q_recv.at[dst], send_sem=q_ssem.at[i],
            recv_sem=q_rsem.at[dst], device_id={"dom": dev}, device_id_type=MESH,
        )

    pl.semaphore_wait(barrier, peers + heads - 2)

    def q_start(i, carry):
        to = ahead(i)
        q_copy(to, to, me, to).start()
        return carry

    lax.fori_loop(1, peers, q_start, 0)
    q_recv[me] = q_send[me]

    a_copy.wait()
    kv_copy.wait()

    def r_copy(i, src, dst, dev):
        return pltpu.make_async_remote_copy(
            src_ref=r_send.at[src], dst_ref=r_recv.at[dst], send_sem=r_ssem.at[i],
            recv_sem=r_rsem.at[dst], device_id={"dom": dev}, device_id_type=MESH,
        )

    per_line = lanes // local
    lane8 = iota((8, ctx), 1)
    row, col = iota((128, 128), 0), iota((128, 128), 1)
    new = col % 16 - 8
    allowed = (row // 16 == col // 16) & (new >= 0) & (new < 4)
    allowed &= ((row % 8) // 4 == new // 2) & (new % 2 <= (row % 4) // 2)

    def attend(group, carry):
        def q_wait(slot, c):
            @pl.when(slot != me)
            def _():
                q_copy(slot, me, slot, slot).wait_recv()

            return c

        lax.fori_loop(group * 8, group * 8 + 8, q_wait, 0)
        slots, parents, scores, messages = [], [], [], []
        for j in range(8):
            slot = group * 8 + j
            parent = a_s[slot // per_line, slot % per_line]
            message = q_recv[slot]
            score = dot_t(message, kv[parent, :, :hd])[:8] * SCORE_SCALE
            scores.append(jnp.where(lane8 < len_s[me * local + parent], score, MASKED_SCORE))
            slots.append(slot)
            parents.append(parent)
            messages.append(message)
        score = jnp.concatenate(scores, axis=0)
        high_c = jnp.max(score, axis=1, keepdims=True)
        expo = jnp.exp(score - high_c)
        total_c = jnp.sum(expo, axis=1, keepdims=True)
        message = jnp.concatenate(messages, axis=0)
        fresh = jnp.where(allowed, dot_t(message, message) * SCORE_SCALE, MASKED_SCORE)
        high_n = jnp.max(fresh, axis=1, keepdims=True)
        expo_n = jnp.exp(fresh - high_n)
        total_n = jnp.sum(expo_n, axis=1, keepdims=True)
        out_n = dot(pltpu.roll(expo_n, 4, 1).astype(BF16), message)

        def queries_of(v):
            return v.reshape(8, 16, v.shape[1])[:, :8].reshape(64, v.shape[1])

        high_n, total_n, out_n = queries_of(high_n), queries_of(total_n), queries_of(out_n)
        highest = jnp.maximum(high_c, high_n)
        factor_c = jnp.exp(high_c - highest)
        factor_n = jnp.exp(high_n - highest)
        total = factor_c * total_c + factor_n * total_n
        for j in range(8):
            at = slice(8 * j, 8 * j + 8)
            out = dot(expo[at].astype(BF16), kv[parents[j], :, hd:])
            out = (factor_c[at] * out + factor_n[at] * out_n[at]) / total[at]
            r_send[slots[j]] = jnp.concatenate(
                [out[:, : hd // 2], out[:, hd // 2 :]], axis=0
            ).astype(BF16)

        def r_start(slot, c):
            @pl.when(slot != me)
            def _():
                r_copy(slot, slot, me, slot).start()

            return c

        lax.fori_loop(group * 8, group * 8 + 8, r_start, 0)
        return carry

    lax.fori_loop(0, peers // 8, attend, 0)
    r_recv[me] = r_send[me]

    def r_wait(i, carry):
        r_copy(i, me, ahead(i), ahead(i)).wait_recv()
        return carry

    lax.fori_loop(1, peers, r_wait, 0)

    back = r_recv[...].astype(F32)
    back = jnp.concatenate(
        [back[:, :8].reshape(8 * peers, hd // 2), back[:, 8:].reshape(8 * peers, hd // 2)], axis=1
    ).astype(BF16)
    attended = dot(scatter, back)
    attended = jnp.concatenate([attended[:rows], attended[rows:]], axis=1).astype(BF16)

    wo_copy.wait()
    step = 256
    quarter = (half // step + 1) // 2 * step
    part = (pl.ds(0, quarter), pl.ds(quarter, half - quarter))

    def around(d):
        return (head + heads + d) % heads

    def to_head(k, src, dst, send_sem, recv_sem, d):
        return pltpu.make_async_remote_copy(
            src_ref=src, dst_ref=dst, send_sem=send_sem.at[k], recv_sem=recv_sem.at[k],
            device_id={"head": around(d)}, device_id_type=MESH,
        )

    def rs_copy(k, src, dst, d):
        return to_head(k, src, dst, rs_ssem, rs_rsem, d)

    ways = ((0, 1), (1, -1))
    plain = [
        rs_copy(k, rs_send.at[around(3 * d), :, part[1 - k]], rs_mid.at[k, :, part[1 - k]], d)
        for k, d in ways
    ]
    fourth = [
        rs_copy(2 + k, rs_send.at[around(4), :, part[k]], rs_half.at[k, :, part[k]], 2 * d)
        for k, d in ways
    ]
    third = [
        rs_copy(4 + k, rs_send.at[around(3 * d), :, part[k]], rs_mid.at[k, :, part[k]], d)
        for k, d in ways
    ]
    direct = [rs_copy(6 + k, rs_send.at[around(d)], rs_recv.at[k], d) for k, d in ways]
    for k in (1, 0):
        for c in range(k * quarter, half if k else quarter, step):
            low = dot(attended, wo[:, c : c + step]).reshape(heads, 8, step)
            upper = dot(attended, wo[:, half + c : half + c + step]).reshape(heads, 8, step)
            rs_send[:, :, c : c + step] = jnp.concatenate([low, upper], axis=1).astype(BF16)
        for copy in (plain[1 - k], fourth[k], third[k]):
            copy.start()
    for copy in direct:
        copy.start()
    late = []

    def hand_on(n, k, d, at, more):
        block = rs_send[around(2 * d), :, at].astype(F32) + rs_mid[k, :, at].astype(F32)
        if more:
            block += rs_half[k, :, at].astype(F32)
        rs_sum[k, :, at] = block.astype(BF16)
        copy = rs_copy(n, rs_sum.at[k, :, at], rs_recv.at[2 + k, :, at], 2 * d)
        copy.start()
        late.append(copy)

    plain[0].wait_recv()
    hand_on(8, 0, 1, part[1], False)
    fourth[1].wait_recv()
    third[1].wait_recv()
    hand_on(11, 1, -1, part[1], True)
    plain[1].wait_recv()
    hand_on(9, 1, -1, part[0], False)
    fourth[0].wait_recv()
    third[0].wait_recv()
    hand_on(10, 0, 1, part[0], True)
    for copy in direct:
        copy.wait_recv()
    projected = rs_send[head].astype(F32) + rs_recv[0].astype(F32) + rs_recv[1].astype(F32)
    for copy in late:
        copy.wait_recv()
    projected += rs_recv[2].astype(F32) + rs_recv[3].astype(F32)

    low, upper = projected[:8], projected[8:]

    def row_scale(a, b):
        square = jnp.sum(a * a, axis=1, keepdims=True) + jnp.sum(b * b, axis=1, keepdims=True)
        return lax.rsqrt(square * (1.0 / width) + EPSILON)

    mine = pl.ds(pl.multiple_of(head * 8, 8), 8)
    scale = row_scale(low, upper)
    low = x32[mine, :half] + low * scale * post_gain[:, :half]
    upper = x32[mine, half:] + upper * scale * post_gain[:, half:]
    scale = row_scale(low, upper)
    twist = jnp.sum(
        low * scale * final_gain[:, :half] * twist_weight[:, :half], axis=1, keepdims=True
    ) + jnp.sum(
        upper * scale * final_gain[:, half:] * twist_weight[:, half:], axis=1, keepdims=True
    )
    lane = iota((8, 128), 1)
    coded = jnp.zeros((8, 128), F32)
    for k, value in enumerate(split3(twist)):
        coded = jnp.where(lane == k, value, coded)
    g_send[:, :half] = jnp.concatenate([low, upper], axis=0).astype(BF16)
    g_send[:, half:] = jnp.concatenate([coded, jnp.zeros((8, 128), F32)], axis=0).astype(BF16)

    def g_copy(k, src, dst, d):
        return to_head(k, src, dst, g_ssem, g_rsem, d)

    part = (pl.ds(0, quarter), pl.ds(quarter, half + 128 - quarter))
    first = [g_copy(k, g_send.at[:, part[k]], g_mid.at[k, :, part[k]], 2 * d) for k, d in ways]
    first += [
        g_copy(2 + k, g_send.at[:, part[1 - k]], g_mid.at[k, :, part[1 - k]], 2 * d)
        for k, d in ways
    ]
    first += [g_copy(4 + k, g_send, g_recv.at[head], d) for k, d in ways]
    for copy in first:
        copy.start()
    own = [pltpu.make_async_copy(g_send, g_recv.at[head], own_sem.at[4])]
    own[0].start()
    second = []
    for n in range(4):
        k, d = ways[n % 2]
        at = part[k] if n < 2 else part[1 - k]
        first[n].wait_recv()
        here, there = g_mid.at[k, :, at], g_recv.at[around(-2 * d), :, at]
        new = [g_copy(6 + k, here, there, 2 * d)] if n < 2 else []
        new.append(g_copy(8 + n, here, there, d))
        for copy in new:
            copy.start()
        second += new
        own.append(pltpu.make_async_copy(here, there, own_sem.at[n]))
        own[-1].start()
    for copy in first[4:] + second:
        copy.wait_recv()
    for copy in own:
        copy.wait()

    def finish_dom(i, carry):
        to = ahead(i)
        q_copy(to, me, me, to).wait_send()
        r_copy(to, me, me, to).wait_send()
        return carry

    lax.fori_loop(1, peers, finish_dom, 0)
    for copy in plain + fourth + third + direct + late + first + second:
        copy.wait_send()


def order_rows(g_ref, out_v, twist_v):
    heads, half = g_ref.shape[0], g_ref.shape[2] - 128
    steps, local = twist_v.shape
    rows = steps * local
    for j in range(0, heads, 2):
        pair = [g_ref[k, :, :half].astype(F32) for k in (j, j + 1)]
        at = slice(8 * j, 8 * j + 16)
        out_v[at, :half] = jnp.concatenate([v[:8] for v in pair], axis=0).astype(BF16)
        out_v[at, half:] = jnp.concatenate([v[8:] for v in pair], axis=0).astype(BF16)
    coded = jnp.concatenate([g_ref[k, :, half:].astype(F32)[:8] for k in range(heads)], axis=0)
    twist = coded[:, 0:1] + coded[:, 1:2] + coded[:, 2:3]
    spread = jnp.where(iota((rows, 128), 0) % local == iota((rows, 128), 1), twist, 0.0)
    twist_v[...] = jnp.sum(spread.reshape(steps, local, 128), axis=1)[:, :local]


def per_device(
    grid3, embeds, ancestors, lengths, kv_cache, attn_gain, w_query, w_keyval, w_out,
    post_gain, final_gain, twist_weight,
):
    steps, local, width = embeds.shape
    ctx, hd2 = kv_cache.shape[1], kv_cache.shape[3]
    peers = lax.axis_size("dom")
    heads = lax.axis_size("head")
    rows = steps * local
    half = width // 2
    lanes = min(128, ancestors.shape[0])
    lines = ancestors.shape[0] // lanes
    vmem = pl.BlockSpec(memory_space=pltpu.VMEM)
    hbm = pl.BlockSpec(memory_space=pltpu.HBM)
    dma = pltpu.SemaphoreType.DMA
    gathered = pl.pallas_call(
        functools.partial(kernel, grid3),
        out_shape=jax.ShapeDtypeStruct((heads, 16, half + 128), BF16),
        in_specs=[hbm, hbm, hbm, hbm, hbm, hbm, hbm, hbm, hbm, hbm, hbm, hbm],
        out_specs=hbm,
        scratch_shapes=[
            pltpu.SMEM(ancestors.shape, jnp.int32),
            pltpu.SMEM(lengths.shape, jnp.int32),
            pltpu.VMEM((lines, lanes), jnp.int32),
            pltpu.VMEM((4, 1, width), F32),
            pltpu.VMEM((rows, width), BF16),
            pltpu.VMEM((rows, width), F32),
            pltpu.VMEM((rows, width), BF16),
            pltpu.VMEM(w_query.shape, BF16),
            pltpu.VMEM(w_keyval.shape, BF16),
            pltpu.VMEM(w_out.shape, BF16),
            pltpu.VMEM((local, ctx, hd2), BF16),
            pltpu.VMEM((lines, lanes), jnp.int32),
            pltpu.SMEM((lines, lanes), jnp.int32),
            pltpu.VMEM((peers, 16, hd2 // 2), BF16),
            pltpu.VMEM((peers, 16, hd2 // 2), BF16),
            pltpu.VMEM((peers, 16, hd2 // 4), BF16),
            pltpu.VMEM((peers, 16, hd2 // 4), BF16),
            pltpu.VMEM((heads, 16, half), BF16),
            pltpu.VMEM((2, 16, half), BF16),
            pltpu.VMEM((2, 16, half), BF16),
            pltpu.VMEM((2, 16, half), BF16),
            pltpu.VMEM((4, 16, half), BF16),
            pltpu.VMEM((16, half + 128), BF16),
            pltpu.VMEM((2, 16, half + 128), BF16),
            dma((3,)), dma((4,)), dma, dma((2, CHUNKS)), dma, dma, dma,
            dma((peers,)), dma((peers,)), dma((peers,)), dma((peers,)),
            dma((12,)), dma((12,)), dma((12,)), dma((12,)), dma((5,)),
        ],
        compiler_params=pltpu.CompilerParams(
            collective_id=0, has_side_effects=True, vmem_limit_bytes=56 * 1024 * 1024
        ),
    )(
        ancestors, lengths, ancestors.reshape(lines, lanes), embeds.reshape(rows, width),
        attn_gain, post_gain,
        final_gain, twist_weight,
        w_query, w_keyval, w_out, kv_cache.reshape(local, ctx, hd2),
    )
    hidden, twist = pl.pallas_call(
        order_rows,
        out_shape=(
            jax.ShapeDtypeStruct((rows, width), BF16),
            jax.ShapeDtypeStruct((steps, local), F32),
        ),
        in_specs=[vmem],
        out_specs=(vmem, vmem),
        compiler_params=pltpu.CompilerParams(vmem_limit_bytes=56 * 1024 * 1024),
    )(gathered)
    return (hidden.reshape(steps, local, width), twist)


def solution(mesh):
    side = math.isqrt(mesh.shape["dom"] // 2)
    grid3 = (mesh.shape["dom"] // (2 * side), side, 2)
    in_specs = (
        P(None, "dom", None), P(), P(), P("dom", None, "head", None), P(), P(None, "head"),
        P(None, "head"), P("head", None), P(), P(), P(),
    )
    out_specs = (P(None, "dom", None), P(None, "dom"))
    return jax.shard_map(
        functools.partial(per_device, grid3), mesh=mesh, in_specs=in_specs, out_specs=out_specs,
        check_vma=False,
    )
```

```python
import functools
import math

import jax
import jax.numpy as jnp
from jax import lax
from jax.experimental import pallas as pl
from jax.experimental.pallas import tpu as pltpu
from jax.sharding import PartitionSpec as P

EPSILON = 1e-06
SCORE_SCALE = 0.0625
MASKED_SCORE = -1e30
LOG_THETA = math.log(10000.0)
MESH = pl.DeviceIdType.MESH
F32 = jnp.float32
BF16 = jnp.bfloat16
CHUNKS = 2


def iota(shape, dim):
    return lax.broadcasted_iota(jnp.int32, shape, dim)


def dot(a, b):
    return jnp.dot(a, b, preferred_element_type=F32)


def dot_t(a, b):
    return lax.dot_general(a, b, (((1,), (1,)), ((), ())), preferred_element_type=F32)


def split3(x):
    high = x.astype(BF16).astype(F32)
    rest = x - high
    mid = rest.astype(BF16).astype(F32)
    return (high, mid, rest - mid)


def kernel(
    grid3, anc_h, len_h, table_h, emb_h, gain_h, post_h, final_h, twist_h,
    wq_h, wkv_h, wo_h, kv_h, g_recv,
    anc_s, len_s, anc_v, gains, emb_b, x32, nrm, wq, wkv, wo, kv, a_v, a_s, q_send, q_recv, r_send, r_recv,
    rs_send, rs_mid, rs_half, rs_sum, rs_recv, g_send, g_mid,
    index_sem, gain_sem, emb_sem, w_sem, wo_sem, kv_sem, a_sem, q_ssem, q_rsem, r_ssem, r_rsem,
    rs_ssem, rs_rsem, g_ssem, g_rsem, own_sem,
):
    ny, nx, nc = grid3
    peers = ny * nx * nc
    local = peers
    heads = rs_send.shape[0]
    rows, width = emb_b.shape
    half = width // 2
    hd = kv.shape[2] // 2
    ctx = kv.shape[1]
    me = lax.axis_index("dom")
    head = lax.axis_index("head")
    my_y, my_x, my_c = me // (nx * nc), (me // nc) % nx, me % nc

    def ahead(i):
        y = (my_y + i // (nx * nc)) % ny
        x = (my_x + (i // nc) % nx) % nx
        return (y * nx + x) * nc + (my_c + i % nc) % nc

    def behind(i):
        y = (my_y + ny - i // (nx * nc)) % ny
        x = (my_x + nx - (i // nc) % nx) % nx
        return (y * nx + x) * nc + (my_c + nc - i % nc) % nc

    index_copies = [
        pltpu.make_async_copy(src, dst, index_sem.at[k])
        for k, (src, dst) in enumerate(((anc_h, anc_s), (len_h, len_s), (table_h, anc_v)))
    ]
    for copy in index_copies:
        copy.start()
    emb_copy = pltpu.make_async_copy(emb_h, emb_b, emb_sem)
    emb_copy.start()
    gain_copies = [
        pltpu.make_async_copy(src, gains.at[k, 0], gain_sem.at[k])
        for k, src in enumerate((gain_h, post_h, final_h, twist_h))
    ]
    for copy in gain_copies:
        copy.start()
    depth = width // CHUNKS
    w_copies = []
    for k, (src, dst) in enumerate(((wq_h, wq), (wkv_h, wkv))):
        part = [pl.ds(c * depth, depth) for c in range(CHUNKS)]
        w_copies.append(
            [pltpu.make_async_copy(src.at[p], dst.at[p], w_sem.at[k, c]) for c, p in enumerate(part)]
        )
    for copy in w_copies[0]:
        copy.start()
    kv_copy = pltpu.make_async_copy(kv_h, kv, kv_sem)
    wo_copy = pltpu.make_async_copy(wo_h, wo, wo_sem)

    barrier = pltpu.get_barrier_semaphore()

    def greet_dom(i, carry):
        pl.semaphore_signal(barrier, inc=1, device_id={"dom": ahead(i)}, device_id_type=MESH)
        return carry

    def greet_head(i, carry):
        pl.semaphore_signal(
            barrier, inc=1, device_id={"head": (head + i) % heads}, device_id_type=MESH
        )
        return carry

    lax.fori_loop(1, peers, greet_dom, 0)
    lax.fori_loop(1, heads, greet_head, 0)

    for copy in index_copies:
        copy.wait()
    table = anc_v[...]
    lines, lanes = table.shape
    lane = iota((lines, lanes), 1)
    hit = jnp.where(table // local == me, table % local, 0)
    picked = jnp.zeros((lines, lanes), jnp.int32)
    for q in range(lanes // local):
        best = jnp.max(jnp.where(lane // local == q, hit, 0), axis=1, keepdims=True)
        picked = jnp.where(lane == q, best, picked)
    a_v[...] = picked
    a_copy = pltpu.make_async_copy(a_v, a_s, a_sem)
    a_copy.start()

    sub = iota((local, 128), 0)
    lane = iota((local, 128), 1)
    source_col = jnp.zeros((local, 128), jnp.int32)
    source_row = jnp.zeros((local, 128), jnp.int32)
    length = jnp.zeros((local, 128), jnp.int32)
    for p in range(local):
        parent = anc_s[me * local + p]
        block = parent // local
        source_col = jnp.where(sub == p, block, source_col)
        source_row = jnp.where(lane % local == p, block, source_row)
        length = jnp.where(sub == p, len_s[parent], length)
    same = source_col == source_row
    rank_row = jnp.sum(jnp.where(same & (sub < lane % local), 1, 0), axis=0, keepdims=True)
    rank_col = jnp.sum(
        jnp.where(same & (lane < sub) & (lane < local), 1, 0), axis=1, keepdims=True
    )
    count = 4 * local
    turn = iota((1, count), 1) // local
    base_row = (source_row[0:1] * 8 + rank_row * 4)[:, :count]
    target_q = base_row + 2 * (turn % 2) + turn // 2
    target_n = source_row[0:1, :count] * 8 + 2 * rank_row[:, :count] + turn % 2 + 4 * (turn // 2)
    slot_row = iota((8 * peers, count), 0)
    gather_q = jnp.where(slot_row == target_q, 1.0, 0.0).astype(BF16)
    gather_n = jnp.where(slot_row == target_n, 1.0, 0.0).astype(BF16)
    base_col = source_col[:, 0:1] * 8 + rank_col * 4
    target_col = jnp.concatenate([base_col + (2 * t + r) for r in range(2) for t in range(2)], 0)
    scatter = jnp.where(iota((count, 8 * peers), 1) == target_col, 1.0, 0.0).astype(BF16)

    position = jnp.concatenate([length, length + 1], axis=0)[:, : hd // 2].astype(F32)
    inverse = jnp.exp(iota((1, hd // 2), 1).astype(F32) * (-LOG_THETA / (hd // 2)))
    angles = position * inverse
    cosine, sine = jnp.cos(angles), jnp.sin(angles)

    def rope(v):
        a, b = v[:, : hd // 2], v[:, hd // 2 :]
        return jnp.concatenate([a * cosine - b * sine, b * cosine + a * sine], axis=1)

    for copy in w_copies[1]:
        copy.start()
    emb_copy.wait()
    for copy in gain_copies:
        copy.wait()
    attn_gain, post_gain, final_gain, twist_weight = (gains.at[k] for k in range(4))

    def norm_rows(i, carry):
        at = pl.ds(pl.multiple_of(i * 16, 16), 16)
        x = emb_b[at, :].astype(F32)
        x32[at, :] = x
        scale = lax.rsqrt(jnp.mean(x * x, axis=1, keepdims=True) + EPSILON)
        nrm[at, :] = (x * scale * attn_gain[...]).astype(BF16)
        return carry

    lax.fori_loop(0, rows // 16, norm_rows, 0)

    @pl.when(head < heads)
    def _():
        for copy in w_copies[0]:
            copy.wait()
        queries = dot(nrm[...], wq[...])
        rotated = jnp.concatenate([rope(queries[:, :hd]), rope(queries[:, hd:])], axis=0)
        q_send[:, :8] = dot(gather_q, rotated.astype(BF16)).reshape(peers, 8, hd).astype(BF16)

    for copy in w_copies[1]:
        copy.wait()
    kv_copy.start()
    wo_copy.start()
    keyval = dot(nrm[...], wkv[...])
    fresh = jnp.concatenate([rope(keyval[:, :hd]), keyval[:, hd:]], axis=0)
    q_send[:, 8:] = dot(gather_n, fresh.astype(BF16)).reshape(peers, 8, hd).astype(BF16)

    def q_copy(i, src, dst, dev):
        return pltpu.make_async_remote_copy(
            src_ref=q_send.at[src], dst_ref=q_recv.at[dst], send_sem=q_ssem.at[i],
            recv_sem=q_rsem.at[dst], device_id={"dom": dev}, device_id_type=MESH,
        )

    pl.semaphore_wait(barrier, peers + heads - 2)

    def q_start(i, carry):
        to = ahead(i)
        q_copy(to, to, me, to).start()
        return carry

    def hops(i):
        y, x = i // (nx * nc), (i // nc) % nx
        return min(y, ny - y) + min(x, nx - x)

    for i in sorted(range(1, peers), key=lambda i: -hops(i)):
        q_start(i, 0)
    q_recv[me] = q_send[me]

    a_copy.wait()
    kv_copy.wait()

    def r_copy(i, src, dst, dev):
        return pltpu.make_async_remote_copy(
            src_ref=r_send.at[src], dst_ref=r_recv.at[dst], send_sem=r_ssem.at[i],
            recv_sem=r_rsem.at[dst], device_id={"dom": dev}, device_id_type=MESH,
        )

    per_line = lanes // local
    lane8 = iota((8, ctx), 1)
    row, col = iota((128, 128), 0), iota((128, 128), 1)
    new = col % 16 - 8
    allowed = (row // 16 == col // 16) & (new >= 0) & (new < 4)
    allowed &= ((row % 8) // 4 == new // 2) & (new % 2 <= (row % 4) // 2)

    def attend(group, carry):
        def q_wait(slot, c):
            @pl.when(slot != me)
            def _():
                q_copy(slot, me, slot, slot).wait_recv()

            return c

        for j in range(8):
            q_wait(group * 8 + j, 0)
        slots, parents, scores, messages = [], [], [], []
        for j in range(8):
            slot = group * 8 + j
            parent = a_s[slot // per_line, slot % per_line]
            message = q_recv[slot]
            score = dot_t(message, kv[parent, :, :hd])[:8] * SCORE_SCALE
            scores.append(jnp.where(lane8 < len_s[me * local + parent], score, MASKED_SCORE))
            slots.append(slot)
            parents.append(parent)
            messages.append(message)
        score = jnp.concatenate(scores, axis=0)
        high_c = jnp.max(score, axis=1, keepdims=True)
        expo = jnp.exp(score - high_c)
        total_c = jnp.sum(expo, axis=1, keepdims=True)
        message = jnp.concatenate(messages, axis=0)
        fresh = jnp.where(allowed, dot_t(message, message) * SCORE_SCALE, MASKED_SCORE)
        high_n = jnp.max(fresh, axis=1, keepdims=True)
        expo_n = jnp.exp(fresh - high_n)
        total_n = jnp.sum(expo_n, axis=1, keepdims=True)
        out_n = dot(pltpu.roll(expo_n, 4, 1).astype(BF16), message)

        def queries_of(v):
            return v.reshape(8, 16, v.shape[1])[:, :8].reshape(64, v.shape[1])

        high_n, total_n, out_n = queries_of(high_n), queries_of(total_n), queries_of(out_n)
        highest = jnp.maximum(high_c, high_n)
        factor_c = jnp.exp(high_c - highest)
        factor_n = jnp.exp(high_n - highest)
        total = factor_c * total_c + factor_n * total_n
        for j in range(8):
            at = slice(8 * j, 8 * j + 8)
            out = dot(expo[at].astype(BF16), kv[parents[j], :, hd:])
            out = (factor_c[at] * out + factor_n[at] * out_n[at]) / total[at]
            r_send[slots[j]] = jnp.concatenate(
                [out[:, : hd // 2], out[:, hd // 2 :]], axis=0
            ).astype(BF16)

        def r_start(slot, c):
            @pl.when(slot != me)
            def _():
                r_copy(slot, slot, me, slot).start()

            return c

        for j in range(8):
            r_start(group * 8 + j, 0)
        return carry

    lax.fori_loop(0, peers // 8, attend, 0)
    r_recv[me] = r_send[me]

    def r_wait(i, carry):
        r_copy(i, me, ahead(i), ahead(i)).wait_recv()
        return carry

    lax.fori_loop(1, peers, r_wait, 0)

    back = r_recv[...].astype(F32)
    back = jnp.concatenate(
        [back[:, :8].reshape(8 * peers, hd // 2), back[:, 8:].reshape(8 * peers, hd // 2)], axis=1
    ).astype(BF16)
    attended = dot(scatter, back)
    attended = jnp.concatenate([attended[:rows], attended[rows:]], axis=1).astype(BF16)

    wo_copy.wait()
    step = 256
    quarter = (half // step + 1) // 2 * step
    part = (pl.ds(0, quarter), pl.ds(quarter, half - quarter))

    def around(d):
        return (head + heads + d) % heads

    def to_head(k, src, dst, send_sem, recv_sem, d):
        return pltpu.make_async_remote_copy(
            src_ref=src, dst_ref=dst, send_sem=send_sem.at[k], recv_sem=recv_sem.at[k],
            device_id={"head": around(d)}, device_id_type=MESH,
        )

    def rs_copy(k, src, dst, d):
        return to_head(k, src, dst, rs_ssem, rs_rsem, d)

    ways = ((0, 1), (1, -1))
    plain = [
        rs_copy(k, rs_send.at[around(3 * d), :, part[1 - k]], rs_mid.at[k, :, part[1 - k]], d)
        for k, d in ways
    ]
    fourth = [
        rs_copy(2 + k, rs_send.at[around(4), :, part[k]], rs_half.at[k, :, part[k]], 2 * d)
        for k, d in ways
    ]
    third = [
        rs_copy(4 + k, rs_send.at[around(3 * d), :, part[k]], rs_mid.at[k, :, part[k]], d)
        for k, d in ways
    ]
    direct = [rs_copy(6 + k, rs_send.at[around(d)], rs_recv.at[k], d) for k, d in ways]
    for k in (1, 0):
        for c in range(k * quarter, half if k else quarter, step):
            low = dot(attended, wo[:, c : c + step]).reshape(heads, 8, step)
            upper = dot(attended, wo[:, half + c : half + c + step]).reshape(heads, 8, step)
            rs_send[:, :, c : c + step] = jnp.concatenate([low, upper], axis=1).astype(BF16)
        for copy in (plain[1 - k], fourth[k], third[k]):
            copy.start()
    for copy in direct:
        copy.start()
    late = []

    def hand_on(n, k, d, at, more):
        block = rs_send[around(2 * d), :, at].astype(F32) + rs_mid[k, :, at].astype(F32)
        if more:
            block += rs_half[k, :, at].astype(F32)
        rs_sum[k, :, at] = block.astype(BF16)
        copy = rs_copy(n, rs_sum.at[k, :, at], rs_recv.at[2 + k, :, at], 2 * d)
        copy.start()
        late.append(copy)

    plain[0].wait_recv()
    hand_on(8, 0, 1, part[1], False)
    fourth[1].wait_recv()
    third[1].wait_recv()
    hand_on(11, 1, -1, part[1], True)
    plain[1].wait_recv()
    hand_on(9, 1, -1, part[0], False)
    fourth[0].wait_recv()
    third[0].wait_recv()
    hand_on(10, 0, 1, part[0], True)
    for copy in direct:
        copy.wait_recv()
    projected = rs_send[head].astype(F32) + rs_recv[0].astype(F32) + rs_recv[1].astype(F32)
    for copy in late:
        copy.wait_recv()
    projected += rs_recv[2].astype(F32) + rs_recv[3].astype(F32)

    low, upper = projected[:8], projected[8:]

    def row_scale(a, b):
        square = jnp.sum(a * a, axis=1, keepdims=True) + jnp.sum(b * b, axis=1, keepdims=True)
        return lax.rsqrt(square * (1.0 / width) + EPSILON)

    mine = pl.ds(pl.multiple_of(head * 8, 8), 8)
    scale = row_scale(low, upper)
    low = x32[mine, :half] + low * scale * post_gain[:, :half]
    upper = x32[mine, half:] + upper * scale * post_gain[:, half:]
    scale = row_scale(low, upper)
    twist = jnp.sum(
        low * scale * final_gain[:, :half] * twist_weight[:, :half], axis=1, keepdims=True
    ) + jnp.sum(
        upper * scale * final_gain[:, half:] * twist_weight[:, half:], axis=1, keepdims=True
    )
    lane = iota((8, 128), 1)
    coded = jnp.zeros((8, 128), F32)
    for k, value in enumerate(split3(twist)):
        coded = jnp.where(lane == k, value, coded)
    g_send[:, :half] = jnp.concatenate([low, upper], axis=0).astype(BF16)
    g_send[:, half:] = jnp.concatenate([coded, jnp.zeros((8, 128), F32)], axis=0).astype(BF16)

    def g_copy(k, src, dst, d):
        return to_head(k, src, dst, g_ssem, g_rsem, d)

    part = (pl.ds(0, quarter), pl.ds(quarter, half + 128 - quarter))
    first = [g_copy(k, g_send.at[:, part[k]], g_mid.at[k, :, part[k]], 2 * d) for k, d in ways]
    first += [
        g_copy(2 + k, g_send.at[:, part[1 - k]], g_mid.at[k, :, part[1 - k]], 2 * d)
        for k, d in ways
    ]
    first += [g_copy(4 + k, g_send, g_recv.at[head], d) for k, d in ways]
    for copy in first:
        copy.start()
    own = [pltpu.make_async_copy(g_send, g_recv.at[head], own_sem.at[4])]
    own[0].start()
    second = []
    for n in range(4):
        k, d = ways[n % 2]
        at = part[k] if n < 2 else part[1 - k]
        first[n].wait_recv()
        here, there = g_mid.at[k, :, at], g_recv.at[around(-2 * d), :, at]
        new = [g_copy(6 + k, here, there, 2 * d)] if n < 2 else []
        new.append(g_copy(8 + n, here, there, d))
        for copy in new:
            copy.start()
        second += new
        own.append(pltpu.make_async_copy(here, there, own_sem.at[n]))
        own[-1].start()
    for copy in first[4:] + second:
        copy.wait_recv()
    for copy in own:
        copy.wait()

    def finish_dom(i, carry):
        to = ahead(i)
        q_copy(to, me, me, to).wait_send()
        r_copy(to, me, me, to).wait_send()
        return carry

    lax.fori_loop(1, peers, finish_dom, 0)
    for copy in plain + fourth + third + direct + late + first + second:
        copy.wait_send()


def order_rows(g_ref, out_v, twist_v):
    heads, half = g_ref.shape[0], g_ref.shape[2] - 128
    steps, local = twist_v.shape
    rows = steps * local
    for j in range(0, heads, 2):
        pair = [g_ref[k, :, :half].astype(F32) for k in (j, j + 1)]
        at = slice(8 * j, 8 * j + 16)
        out_v[at, :half] = jnp.concatenate([v[:8] for v in pair], axis=0).astype(BF16)
        out_v[at, half:] = jnp.concatenate([v[8:] for v in pair], axis=0).astype(BF16)
    coded = jnp.concatenate([g_ref[k, :, half:].astype(F32)[:8] for k in range(heads)], axis=0)
    twist = coded[:, 0:1] + coded[:, 1:2] + coded[:, 2:3]
    spread = jnp.where(iota((rows, 128), 0) % local == iota((rows, 128), 1), twist, 0.0)
    twist_v[...] = jnp.sum(spread.reshape(steps, local, 128), axis=1)[:, :local]


def per_device(
    grid3, embeds, ancestors, lengths, kv_cache, attn_gain, w_query, w_keyval, w_out,
    post_gain, final_gain, twist_weight,
):
    steps, local, width = embeds.shape
    ctx, hd2 = kv_cache.shape[1], kv_cache.shape[3]
    peers = lax.axis_size("dom")
    heads = lax.axis_size("head")
    rows = steps * local
    half = width // 2
    lanes = min(128, ancestors.shape[0])
    lines = ancestors.shape[0] // lanes
    vmem = pl.BlockSpec(memory_space=pltpu.VMEM)
    hbm = pl.BlockSpec(memory_space=pltpu.HBM)
    dma = pltpu.SemaphoreType.DMA
    gathered = pl.pallas_call(
        functools.partial(kernel, grid3),
        out_shape=jax.ShapeDtypeStruct((heads, 16, half + 128), BF16),
        in_specs=[hbm, hbm, hbm, hbm, hbm, hbm, hbm, hbm, hbm, hbm, hbm, hbm],
        out_specs=hbm,
        scratch_shapes=[
            pltpu.SMEM(ancestors.shape, jnp.int32),
            pltpu.SMEM(lengths.shape, jnp.int32),
            pltpu.VMEM((lines, lanes), jnp.int32),
            pltpu.VMEM((4, 1, width), F32),
            pltpu.VMEM((rows, width), BF16),
            pltpu.VMEM((rows, width), F32),
            pltpu.VMEM((rows, width), BF16),
            pltpu.VMEM(w_query.shape, BF16),
            pltpu.VMEM(w_keyval.shape, BF16),
            pltpu.VMEM(w_out.shape, BF16),
            pltpu.VMEM((local, ctx, hd2), BF16),
            pltpu.VMEM((lines, lanes), jnp.int32),
            pltpu.SMEM((lines, lanes), jnp.int32),
            pltpu.VMEM((peers, 16, hd2 // 2), BF16),
            pltpu.VMEM((peers, 16, hd2 // 2), BF16),
            pltpu.VMEM((peers, 16, hd2 // 4), BF16),
            pltpu.VMEM((peers, 16, hd2 // 4), BF16),
            pltpu.VMEM((heads, 16, half), BF16),
            pltpu.VMEM((2, 16, half), BF16),
            pltpu.VMEM((2, 16, half), BF16),
            pltpu.VMEM((2, 16, half), BF16),
            pltpu.VMEM((4, 16, half), BF16),
            pltpu.VMEM((16, half + 128), BF16),
            pltpu.VMEM((2, 16, half + 128), BF16),
            dma((3,)), dma((4,)), dma, dma((2, CHUNKS)), dma, dma, dma,
            dma((peers,)), dma((peers,)), dma((peers,)), dma((peers,)),
            dma((12,)), dma((12,)), dma((12,)), dma((12,)), dma((5,)),
        ],
        compiler_params=pltpu.CompilerParams(
            collective_id=0, has_side_effects=True, vmem_limit_bytes=56 * 1024 * 1024
        ),
    )(
        ancestors, lengths, ancestors.reshape(lines, lanes), embeds.reshape(rows, width),
        attn_gain, post_gain,
        final_gain, twist_weight,
        w_query, w_keyval, w_out, kv_cache.reshape(local, ctx, hd2),
    )
    hidden, twist = pl.pallas_call(
        order_rows,
        out_shape=(
            jax.ShapeDtypeStruct((rows, width), BF16),
            jax.ShapeDtypeStruct((steps, local), F32),
        ),
        in_specs=[vmem],
        out_specs=(vmem, vmem),
        compiler_params=pltpu.CompilerParams(vmem_limit_bytes=56 * 1024 * 1024),
    )(gathered)
    return (hidden.reshape(steps, local, width), twist)


def solution(mesh):
    side = math.isqrt(mesh.shape["dom"] // 2)
    grid3 = (mesh.shape["dom"] // (2 * side), side, 2)
    in_specs = (
        P(None, "dom", None), P(), P(), P("dom", None, "head", None), P(), P(None, "head"),
        P(None, "head"), P("head", None), P(), P(), P(),
    )
    out_specs = (P(None, "dom", None), P(None, "dom"))
    return jax.shard_map(
        functools.partial(per_device, grid3), mesh=mesh, in_specs=in_specs, out_specs=out_specs,
        check_vma=False,
    )
```
